32 devices in a mesh: chain: 8 (over z, y), group: 4 (over x, core).
Axes of the slice: x: 2, y: 2, z: 4, core: 2. Of those that a mesh axis runs over, the one named last changes fastest.
Arguments:
- site_tensors: bfloat16 [4, 8, 16, 256, 2, 256], P('group', 'chain')
- bond_weights: float32 [4, 8, 16, 256], P('group', 'chain'), may hold values from 0.5 to 1.5
- sector_sizes: int32 [4, 8, 16], P('group', 'chain'), may hold values from 192 to 256, as said below
- kept_ranks: int32 [4, 8, 16], P('group', 'chain'), may hold values from 128 to 256, as said below
- sketches: bfloat16 [16, 512, 256], replicated, may hold values from -6 to 6
- gate_ends: float32 [2], replicated, may hold values from 0.5 to 1.5
- gate_pair: float32 [3], replicated, may hold values from -0.4 to 0.4
Outputs:
- updated_sites: bfloat16 [4, 8, 16, 256, 2, 256], P('group', 'chain')
The draws below stay inside these ranges and needn't reach their ends.
Inputs may be any that keep to these rules, and one draw needn't show every extreme that they name: `sector_sizes`: every bond has one charge sector, the same for all bonds of a draw, of size 256. `kept_ranks`: A kept rank of sector q of bond n is at most the size of sector q of bonds n - 1, n and n + 1 (bonds outside the MPS count as 256); in the sector of size 256 it equals 256.
All inputs are finite; a program needn't handle non-finite values.
Results may differ from the reference program's by a relative error of at most 0.0088.
Values may be sent and summed in bfloat16 or wider, within the bound.
A program may use at most 192 MiB of HBM per device.

```python
import math
import jax
import jax.numpy as jnp
from jax import lax

NQ = 16
B = 256
SEGMENTS = 4
CHAIN_DEV = 8


def sector_plan(key):
    seeded = jax.random.fold_in(key, 4099)
    site_count = SEGMENTS * CHAIN_DEV
    sector_dims = jax.random.randint(jax.random.fold_in(seeded, 1), (site_count, NQ), 3 * B // 4, B + 1)
    full_sector = jax.random.randint(jax.random.fold_in(seeded, 2), (), 0, NQ)
    column = lax.broadcasted_iota(jnp.int32, (site_count, NQ), 1)
    sector_dims = jnp.where(column == full_sector, B, sector_dims)
    boundary = jnp.full((1, NQ), B, jnp.int32)
    earlier = jnp.concatenate([boundary, sector_dims[:-1]], axis=0)
    later_dims = jnp.concatenate([sector_dims[1:], boundary], axis=0)
    picked = jax.random.randint(jax.random.fold_in(seeded, 3), (site_count, NQ), B // 2, B + 1)
    kept = jnp.minimum(jnp.minimum(picked, sector_dims), jnp.minimum(earlier, later_dims))
    kept = jnp.where(column == full_sector, B, kept)
    return (sector_dims.reshape(SEGMENTS, CHAIN_DEV, NQ), kept.reshape(SEGMENTS, CHAIN_DEV, NQ))


def draw_sector_sizes(key, part):
    return sector_plan(key)[0]


def draw_kept_ranks(key, part):
    return sector_plan(key)[1]


def draw_site_tensors(key, part):
    shape = (SEGMENTS, CHAIN_DEV, NQ, B, 2, B)
    noise = jax.random.normal(jax.random.fold_in(key, 11), shape, jnp.float32)
    noise = noise * (0.8 / B ** 0.5)
    diagonal = jax.random.uniform(jax.random.fold_in(key, 12), (SEGMENTS, CHAIN_DEV, NQ, 1, 2, B), jnp.float32, 1.0, 2.0)
    rows = lax.broadcasted_iota(jnp.int32, (1, 1, 1, B, 1, B), 3)
    cols = lax.broadcasted_iota(jnp.int32, (1, 1, 1, B, 1, B), 5)
    identity = (rows == cols).astype(jnp.float32)
    return (noise + diagonal * identity).astype(jnp.bfloat16)


def level_of(own_key, shape, cuts, least, high):
    level = 1.0
    for position, shards_of in cuts:
        steps = jax.random.uniform(jax.random.fold_in(jax.random.fold_in(own_key, 6), position), (shards_of,), jnp.float32, least / len(cuts), high / len(cuts))
        level = level * jnp.repeat(jnp.exp(steps), shape[position] // shards_of).reshape((-1,) + (1,) * (len(shape) - 1 - position))
    return level


def gaussian(key, extent, scale, reach, held_as=jnp.bfloat16):
    return jnp.clip(scale * jax.random.normal(key, extent, jnp.float32), -reach, reach).astype(held_as)


def setup_inputs(seed: int = 0) -> dict:
    keys = jax.random.split(jax.random.key(seed), 8)
    site_tensors = draw_site_tensors(jax.random.fold_in(keys[7], 71), 0)
    bond_weights = jnp.clip(jnp.exp(math.log(1.5) - 1.0986123 * jax.random.uniform(keys[1], (SEGMENTS, CHAIN_DEV, NQ, B), jnp.float32) ** level_of(keys[1], (SEGMENTS, CHAIN_DEV, NQ, B), ((0, 4), (1, 8)), -0.2, 0.2)), 0.5, 1.5)
    sector_sizes = draw_sector_sizes(jax.random.fold_in(keys[7], 71), 0)
    kept_ranks = draw_kept_ranks(jax.random.fold_in(keys[7], 71), 0)
    sketches = gaussian(keys[4], (NQ, 2 * B, B), 1.0, 6.0)
    gate_ends = jnp.clip(jnp.exp(jax.random.uniform(keys[5], (2,), jnp.float32, math.log(0.5), math.log(1.5))), 0.5, 1.5)
    gate_pair = jnp.clip(jax.random.uniform(keys[6], (3,), jnp.float32, -0.4, 0.4), -0.4, 0.4)
    return dict(site_tensors=site_tensors, bond_weights=bond_weights, sector_sizes=sector_sizes, kept_ranks=kept_ranks, sketches=sketches, gate_ends=gate_ends, gate_pair=gate_pair)


def shift_next(values):
    return jnp.concatenate([values[1:], jnp.zeros_like(values[:1])], axis=0)

def shift_prev(values):
    return jnp.concatenate([jnp.zeros_like(values[:1]), values[:-1]], axis=0)

def weigh_tensor(tensor, row_lam, col_lam):
    col_scale = jnp.stack([col_lam, shift_next(col_lam)], axis=1)
    scaled = tensor.astype(jnp.float32) * row_lam[:, :, None, None]
    return (scaled * col_scale[:, None, :, :]).astype(jnp.bfloat16)

def truncate_bond(two_site, kept_mask, sketch_win, gate_ends, gate_pair):
    middle = two_site[1:-1]
    block_zz = gate_ends[0] * middle[:, 0, :, 0, :]
    block_oo = gate_ends[1] * middle[:, 1, :, 1, :]
    block_zo = (1.0 + gate_pair[0]) * middle[:, 0, :, 1, :] + gate_pair[2] * two_site[2:, 1, :, 0, :]
    block_oz = gate_pair[2] * two_site[:-2, 0, :, 1, :] + (1.0 + gate_pair[1]) * middle[:, 1, :, 0, :]
    upper = jnp.concatenate([block_zz, block_zo], axis=-1)
    lower = jnp.concatenate([block_oz, block_oo], axis=-1)
    mixed = jnp.concatenate([upper, lower], axis=1).astype(jnp.bfloat16)
    block_size = kept_mask.shape[1]
    sketch_cols = sketch_win * kept_mask[:, None, :]
    sampled = jnp.einsum('mij,mjk->mik', mixed.astype(jnp.float32), sketch_cols.astype(jnp.float32), precision=lax.Precision.HIGHEST)
    gram_matrix = jnp.einsum('mik,mil->mkl', sampled, sampled, precision=lax.Precision.HIGHEST)
    shift_amount = 0.01 * lax.optimization_barrier(jnp.sum(sampled * sampled, axis=(1, 2))) / block_size
    diag_add = 1.0 - kept_mask.astype(jnp.float32) + shift_amount[:, None]
    gram_matrix = gram_matrix + diag_add[:, :, None] * jnp.eye(block_size, dtype=jnp.float32)[None]
    lower_factor = jnp.linalg.cholesky(gram_matrix)
    factor_t = jax.scipy.linalg.solve_triangular(lower_factor, jnp.swapaxes(sampled, 1, 2), lower=True)
    scaled = (factor_t * math.sqrt(block_size)).astype(jnp.bfloat16)
    right_part = jnp.einsum('mki,mij->mkj', scaled.astype(jnp.float32), mixed.astype(jnp.float32), precision=lax.Precision.HIGHEST)
    right_part = (right_part / block_size).astype(jnp.bfloat16)
    return (scaled, right_part)

def left_from_factor(scaled):
    block_size = scaled.shape[1]
    columns = jnp.swapaxes(scaled, 1, 2)
    upper = columns[:, :block_size, :]
    lower = shift_next(columns[:, block_size:, :])
    return jnp.stack([upper, lower], axis=2)

def reference(site_tensors, bond_weights, sector_sizes, kept_ranks, sketches, gate_ends, gate_pair):
    site_count = SEGMENTS * CHAIN_DEV
    pair_count = site_count // 2
    column = lax.broadcasted_iota(jnp.int32, (NQ, B), 1)
    sites = site_tensors.reshape(site_count, NQ, B, 2, B)
    lam = bond_weights.reshape(site_count, NQ, B) * (column[None] < sector_sizes.reshape(site_count, NQ)[:, :, None]).astype(jnp.float32)
    kept_mask = (column[None] < kept_ranks.reshape(site_count, NQ)[:, :, None]).astype(jnp.bfloat16)
    lam_left = jnp.concatenate([jnp.ones((1, NQ, B), jnp.float32), lam[:-1]], axis=0)

    def one_pair(pair_inputs):
        pair_sites, pair_lam, left_lam, pair_kept = pair_inputs
        left_w = weigh_tensor(pair_sites[0], left_lam[0], jnp.ones((NQ, B), jnp.float32))
        right_w = weigh_tensor(pair_sites[1], left_lam[1], pair_lam[1])
        left_block = jnp.concatenate([left_w[:, :, 0, :], shift_prev(left_w[:, :, 1, :])], axis=1)
        right_block = right_w.reshape(NQ, B, 2 * B)
        two_site = jnp.einsum('mik,mkj->mij', left_block.astype(jnp.float32), right_block.astype(jnp.float32), precision=lax.Precision.HIGHEST)
        two_site = two_site.reshape(NQ, 2, B, 2, B)
        zero_sector = jnp.zeros((1, 2, B, 2, B), jnp.float32)
        two_site = jnp.concatenate([zero_sector, two_site, zero_sector], axis=0)
        scaled, right_part = truncate_bond(two_site, pair_kept[0], sketches, gate_ends, gate_pair)
        return jnp.stack([left_from_factor(scaled), right_part.reshape(NQ, B, 2, B)], axis=0)
    updated = lax.map(one_pair, (sites.reshape(pair_count, 2, NQ, B, 2, B), lam.reshape(pair_count, 2, NQ, B), lam_left.reshape(pair_count, 2, NQ, B), kept_mask.reshape(pair_count, 2, NQ, B)))
    return updated.reshape(SEGMENTS, CHAIN_DEV, NQ, B, 2, B)
```

```python
import functools
import math

import jax
import jax.numpy as jnp
from jax import lax
from jax.experimental import pallas as pl
from jax.experimental.pallas import tpu as pltpu
from jax.sharding import PartitionSpec as P

CHUNKS = 2
NB = 64
NN = (((1,), (0,)), ((), ()))
NT = (((1,), (1,)), ((), ()))
TN = (((0,), (0,)), ((), ()))


def dot(a, b, dims=NN):
    return lax.dot_general(a, b, dims, preferred_element_type=jnp.float32)


def halves(x):
    high = x.astype(jnp.bfloat16)
    return high, (x - high.astype(jnp.float32)).astype(jnp.bfloat16)


def dot3(a, b, dims=NN):
    (ah, al), (bh, bl) = a, b
    return dot(ah, bh, dims) + (dot(ah, bl, dims) + dot(al, bh, dims))


def inverse_factors(blocks):
    tiles = NB // 8
    sub = lax.broadcasted_iota(jnp.int32, (8, 2 * NB), 0)
    lane = lax.broadcasted_iota(jnp.int32, (8, 2 * NB), 1)
    work = []
    for block in blocks:
        rows = []
        for t in range(tiles):
            one = (lane == sub + (NB + 8 * t)).astype(jnp.float32)
            wide = jnp.concatenate([block[8 * t : 8 * t + 8], jnp.zeros((8, NB), jnp.float32)], axis=1)
            rows.append(wide + one)
        work.append(rows)
    for k in range(NB):
        at, inside = k // 8, k % 8
        for rows in work:
            first = jnp.broadcast_to(rows[at][:, k : k + 1], (8, 2 * NB))
            pivot = jnp.broadcast_to(first[inside : inside + 1], (8, 2 * NB))
            line = jnp.broadcast_to(rows[at][inside : inside + 1], (8, 2 * NB)) / pivot
            for t in range(at + 1, tiles):
                rows[t] = rows[t] - jnp.broadcast_to(rows[t][:, k : k + 1], (8, 2 * NB)) * line
            if inside < 7:
                rows[at] = rows[at] - jnp.where(sub > inside, first, 0.0) * line
    found = []
    for rows in work:
        scaled = []
        for t in range(tiles):
            diag = jnp.sum(jnp.where(lane == sub + 8 * t, rows[t], 0.0), axis=1, keepdims=True)
            scaled.append(rows[t] * lax.rsqrt(diag))
        found.append(jnp.concatenate(scaled, axis=0)[:, NB:])
    return found


def truncate_kernel(side_ref, gates_ref, own0, own1, got0, got1, kept_ref, sketch_ref,
                    keep_ref, send_ref, mixed_ref, sampled_ref, work_ref):
    count, _, size, _ = keep_ref.shape
    is_right = side_ref[0] == 1
    end0, end1 = gates_ref[0], gates_ref[1]
    p0, p1, p2 = gates_ref[2], gates_ref[3], gates_ref[4]
    eye = lax.broadcasted_iota(jnp.int32, (size, size), 0) == lax.broadcasted_iota(
        jnp.int32, (size, size), 1
    )

    def left(own, got, t):
        return jnp.where(is_right, got[t], own[t])

    def right(own, got, t):
        return jnp.where(is_right, own[t], got[t])

    def prepare(t, carry):
        l0_prev, l0 = left(own0, got0, t), left(own0, got0, t + 1)
        l1_prev, l1 = left(own1, got1, t), left(own1, got1, t + 1)
        r0, r0_next = right(own0, got0, t), right(own0, got0, t + 1)
        r1_prev, r1 = right(own1, got1, t), right(own1, got1, t + 1)
        z00 = end0 * dot(l0, r0)
        z01 = (1.0 + p0) * dot(l0, r1) + p2 * dot(l1, r0_next)
        z10 = p2 * dot(l0_prev, r1_prev) + (1.0 + p1) * dot(l1_prev, r0)
        z11 = end1 * dot(l1_prev, r1)
        mixed_ref[t, :size, :size] = z00.astype(jnp.bfloat16)
        mixed_ref[t, :size, size:] = z01.astype(jnp.bfloat16)
        mixed_ref[t, size:, :size] = z10.astype(jnp.bfloat16)
        mixed_ref[t, size:, size:] = z11.astype(jnp.bfloat16)
        kept = kept_ref[t]
        sampled = dot(mixed_ref[t], sketch_ref[t] * kept.astype(jnp.bfloat16))
        sampled_ref[t] = sampled
        parts = halves(sampled)
        gram = dot3(parts, parts, TN)
        shift = 0.01 * jnp.sum(sampled * sampled) / size
        work_ref[t, :, :size] = gram + jnp.where(eye, (1.0 - kept) + shift, 0.0)
        work_ref[t, :, size:] = eye.astype(jnp.float32)
        return carry

    lax.fori_loop(0, count, prepare, 0)
    for low in range(0, size, NB):
        high = low + NB
        found = inverse_factors([work_ref[t, low:high, low:high] for t in range(count)])
        for t in range(count):
            rows = dot3(halves(found[t]), halves(work_ref[t, low:high, :]))
            work_ref[t, low:high, :] = rows
            if high < size:
                rh, rl = halves(rows)
                update = dot3((rh[:, high:size], rl[:, high:size]), (rh, rl), TN)
                work_ref[t, high:, :] = work_ref[t, high:, :] - update

    def finish(t, carry):
        inverse = halves(work_ref[t, :, size:])
        scaled = math.sqrt(size) * dot3(inverse, halves(sampled_ref[t]), NT)
        rounded = scaled.astype(jnp.bfloat16)
        right_part = (dot(rounded, mixed_ref[t]) / size).astype(jnp.bfloat16)
        columns = scaled.T.astype(jnp.bfloat16)
        for s in range(2):
            up = columns[s * size : (s + 1) * size]
            part = right_part[:, s * size : (s + 1) * size]
            keep_ref[t, s] = jnp.where(is_right, part, up)
            send_ref[t, s] = jnp.where(is_right, up, part)
        return carry

    lax.fori_loop(0, count, finish, 0)


def truncate(side, gates, own0, own1, got0, got1, kept, sketch):
    count, rows, size = sketch.shape
    vmem = pl.BlockSpec(memory_space=pltpu.VMEM)
    smem = pl.BlockSpec(memory_space=pltpu.SMEM)
    shape = jax.ShapeDtypeStruct((count, 2, size, size), jnp.bfloat16)
    return pl.pallas_call(
        truncate_kernel,
        out_shape=(shape, shape),
        in_specs=[smem, smem] + [vmem] * 6,
        out_specs=(vmem, vmem),
        scratch_shapes=[
            pltpu.VMEM((count, rows, rows), jnp.bfloat16),
            pltpu.VMEM((count, rows, size), jnp.float32),
            pltpu.VMEM((count, size, 2 * size), jnp.float32),
        ],
        compiler_params=pltpu.CompilerParams(vmem_limit_bytes=48 * 2**20),
        cost_estimate=pl.CostEstimate(
            flops=count * 100 * size**3, bytes_accessed=count * 8 * size * size * 8, transcendentals=0
        ),
    )(side, gates, own0, own1, got0, got1, kept, sketch)


def from_partner(value):
    pairs = [(source, source ^ 1) for source in range(lax.axis_size("chain"))]
    return lax.ppermute(value, "chain", pairs)


def from_previous_site(value):
    groups, chain = lax.axis_size("group"), lax.axis_size("chain")
    at = [c * groups + g for g in range(groups) for c in range(chain)]
    return lax.ppermute(value, ("chain", "group"), list(zip(at[:-1], at[1:])))


def shift_next(values):
    return jnp.concatenate([values[1:], jnp.zeros_like(values[:1])], axis=0)


def shards(site_tensors, bond_weights, sector_sizes, kept_ranks, sketches, gate_ends, gate_pair):
    own_site = site_tensors[0, 0]
    nq, size = own_site.shape[:2]
    chain_at = lax.axis_index("chain")
    group_at = lax.axis_index("group")
    is_right = chain_at % 2 == 1
    column = lax.broadcasted_iota(jnp.int32, (nq, size), 1)
    own_lam = bond_weights[0, 0] * (column < sector_sizes[0, 0][:, None]).astype(jnp.float32)
    kept_own = (column < kept_ranks[0, 0][:, None]).astype(jnp.float32)
    message = from_previous_site(jnp.stack([own_lam, kept_own]))
    all_ones = jnp.ones((nq, size), jnp.float32)
    row_scale = jnp.where((chain_at == 0) & (group_at == 0), all_ones, message[0])
    kept_mask = jnp.where(is_right, message[1], kept_own)
    col_lam = jnp.where(is_right, own_lam, all_ones)
    col_next = shift_next(col_lam)

    def weigh(s, scale):
        value = own_site[:, :, s, :].astype(jnp.float32) * row_scale[:, :, None]
        return jnp.pad((value * scale[:, None, :]).astype(jnp.bfloat16), ((1, 1), (0, 0), (0, 0)))

    padded0, padded1 = weigh(0, col_lam), weigh(1, col_next)
    sectors = nq // 2
    each = sectors // CHUNKS
    send0 = jnp.where(is_right, 1, sectors)
    send1 = jnp.where(is_right, 0, sectors)
    mine0 = jnp.where(is_right, sectors + 1, 0)
    mine1 = jnp.where(is_right, sectors, 0)
    first = jnp.where(is_right, sectors, 0)
    cut = functools.partial(lax.dynamic_slice_in_dim, axis=0)

    side = is_right.astype(jnp.int32)[None]
    gates = jnp.concatenate([gate_ends, gate_pair])
    got = []
    for c in range(CHUNKS):
        low = 0 if c == 0 else c * each + 1
        length = (c + 1) * each + 1 - low
        got.append(from_partner((cut(padded0, send0 + low, length), cut(padded1, send1 + low, length))))
    kept_parts, back_parts = [], []
    for c in range(CHUNKS):
        if c == 0:
            got0, got1 = got[0]
        else:
            got0 = jnp.concatenate([got[c - 1][0][-1:], got[c][0]])
            got1 = jnp.concatenate([got[c - 1][1][-1:], got[c][1]])
        start = c * each
        keep, send = truncate(
            side,
            gates,
            cut(padded0, mine0 + start, each + 1),
            cut(padded1, mine1 + start, each + 1),
            got0,
            got1,
            cut(kept_mask, first + start, each)[:, None, :],
            cut(sketches, first + start, each),
        )
        kept_parts.append(keep)
        back_parts.append(from_partner(send))
    keep = jnp.concatenate(kept_parts)
    back = jnp.concatenate(back_parts)
    whole = jnp.where(
        is_right, jnp.concatenate([back, keep]), jnp.concatenate([keep, back])
    )
    second = jnp.where(is_right, whole[:, 1], shift_next(whole[:, 1]))
    return jnp.stack([whole[:, 0], second], axis=2)[None, None]


def solution(mesh):
    return jax.shard_map(
        shards,
        mesh=mesh,
        in_specs=(
            P("group", "chain", None, None, None, None),
            P("group", "chain", None, None),
            P("group", "chain", None),
            P("group", "chain", None),
            P(),
            P(),
            P(),
        ),
        out_specs=P("group", "chain", None, None, None, None),
        check_vma=False,
    )
```

```python
import functools
import math

import jax
import jax.numpy as jnp
from jax import lax
from jax.experimental import pallas as pl
from jax.experimental.pallas import tpu as pltpu
from jax.sharding import PartitionSpec as P

CHUNKS = 2
NB = 64
GROUP = 4
NN = (((1,), (0,)), ((), ()))
NT = (((1,), (1,)), ((), ()))
TN = (((0,), (0,)), ((), ()))


def dot(a, b, dims=NN):
    return lax.dot_general(a, b, dims, preferred_element_type=jnp.float32)


def halves(x):
    high = x.astype(jnp.bfloat16)
    return high, (x - high.astype(jnp.float32)).astype(jnp.bfloat16)


def dot3(a, b, dims=NN):
    (ah, al), (bh, bl) = a, b
    return dot(ah, bh, dims) + (dot(ah, bl, dims) + dot(al, bh, dims))


def inverse_factors(blocks):
    tiles = NB // 8
    sub = lax.broadcasted_iota(jnp.int32, (8, 2 * NB), 0)
    lane = lax.broadcasted_iota(jnp.int32, (8, 2 * NB), 1)
    work = []
    for block in blocks:
        rows = []
        for t in range(tiles):
            one = (lane == sub + (NB + 8 * t)).astype(jnp.float32)
            wide = jnp.concatenate([block[8 * t : 8 * t + 8], jnp.zeros((8, NB), jnp.float32)], axis=1)
            rows.append(wide + one)
        work.append(rows)
    def across(row):
        return jnp.broadcast_to(row, (8, 2 * NB))

    for k in range(0, NB, GROUP):
        at, inside = k // 8, k % 8
        for rows in work:
            cols = [
                {t: across(rows[t][:, k + j : k + j + 1]) for t in range(at, tiles)} for j in range(GROUP)
            ]
            for j in range(GROUP):
                row = inside + j
                inverse = 1.0 / across(cols[j][at][row : row + 1])
                line = across(rows[at][row : row + 1]) * inverse
                ratio = [across(cols[i][at][row : row + 1]) * inverse for i in range(j + 1, GROUP)]
                for t in range(at, tiles):
                    if t == at and row == 7:
                        continue
                    column = jnp.where(sub > row, cols[j][t], 0.0) if t == at else cols[j][t]
                    for i in range(j + 1, GROUP):
                        cols[i][t] = cols[i][t] - column * ratio[i - j - 1]
                    rows[t] = rows[t] - column * line
    found = []
    for rows in work:
        scaled = []
        for t in range(tiles):
            diag = jnp.sum(jnp.where(lane == sub + 8 * t, rows[t], 0.0), axis=1, keepdims=True)
            scaled.append(rows[t] * lax.rsqrt(diag))
        found.append(jnp.concatenate(scaled, axis=0)[:, NB:])
    return found


def truncate_kernel(side_ref, gates_ref, own0, own1, got0, got1, kept_ref, sketch_ref,
                    keep_ref, send_ref, mixed_ref, sampled_ref, work_ref):
    count, _, size, _ = keep_ref.shape
    is_right = side_ref[0] == 1
    end0, end1 = gates_ref[0], gates_ref[1]
    p0, p1, p2 = gates_ref[2], gates_ref[3], gates_ref[4]
    eye = lax.broadcasted_iota(jnp.int32, (size, size), 0) == lax.broadcasted_iota(
        jnp.int32, (size, size), 1
    )

    def left(own, got, t):
        return jnp.where(is_right, got[t], own[t])

    def right(own, got, t):
        return jnp.where(is_right, own[t], got[t])

    def prepare(t, carry):
        l0_prev, l0 = left(own0, got0, t), left(own0, got0, t + 1)
        l1_prev, l1 = left(own1, got1, t), left(own1, got1, t + 1)
        r0, r0_next = right(own0, got0, t), right(own0, got0, t + 1)
        r1_prev, r1 = right(own1, got1, t), right(own1, got1, t + 1)
        z00 = end0 * dot(l0, r0)
        z01 = (1.0 + p0) * dot(l0, r1) + p2 * dot(l1, r0_next)
        z10 = p2 * dot(l0_prev, r1_prev) + (1.0 + p1) * dot(l1_prev, r0)
        z11 = end1 * dot(l1_prev, r1)
        mixed_ref[t, :size, :size] = z00.astype(jnp.bfloat16)
        mixed_ref[t, :size, size:] = z01.astype(jnp.bfloat16)
        mixed_ref[t, size:, :size] = z10.astype(jnp.bfloat16)
        mixed_ref[t, size:, size:] = z11.astype(jnp.bfloat16)
        kept = kept_ref[t]
        sampled = dot(mixed_ref[t], sketch_ref[t] * kept.astype(jnp.bfloat16))
        sampled_ref[t] = sampled
        parts = halves(sampled)
        gram = dot3(parts, parts, TN)
        shift = 0.01 * jnp.sum(sampled * sampled) / size
        work_ref[t, :, :size] = gram + jnp.where(eye, (1.0 - kept) + shift, 0.0)
        work_ref[t, :, size:] = eye.astype(jnp.float32)
        return carry

    lax.fori_loop(0, count, prepare, 0)
    for low in range(0, size, NB):
        high = low + NB
        found = inverse_factors([work_ref[t, low:high, low:high] for t in range(count)])
        for t in range(count):
            rows = dot3(halves(found[t]), halves(work_ref[t, low:high, :]))
            work_ref[t, low:high, :] = rows
            if high < size:
                rh, rl = halves(rows)
                update = dot3((rh[:, high:size], rl[:, high:size]), (rh, rl), TN)
                work_ref[t, high:, :] = work_ref[t, high:, :] - update

    def finish(t, carry):
        inverse = halves(work_ref[t, :, size:])
        scaled = math.sqrt(size) * dot3(inverse, halves(sampled_ref[t]), NT)
        rounded = scaled.astype(jnp.bfloat16)
        right_part = (dot(rounded, mixed_ref[t]) / size).astype(jnp.bfloat16)
        columns = scaled.T.astype(jnp.bfloat16)
        for s in range(2):
            up = columns[s * size : (s + 1) * size]
            part = right_part[:, s * size : (s + 1) * size]
            keep_ref[t, s] = jnp.where(is_right, part, up)
            send_ref[t, s] = jnp.where(is_right, up, part)
        return carry

    lax.fori_loop(0, count, finish, 0)


def truncate(side, gates, own0, own1, got0, got1, kept, sketch):
    count, rows, size = sketch.shape
    vmem = pl.BlockSpec(memory_space=pltpu.VMEM)
    smem = pl.BlockSpec(memory_space=pltpu.SMEM)
    shape = jax.ShapeDtypeStruct((count, 2, size, size), jnp.bfloat16)
    return pl.pallas_call(
        truncate_kernel,
        out_shape=(shape, shape),
        in_specs=[smem, smem] + [vmem] * 6,
        out_specs=(vmem, vmem),
        scratch_shapes=[
            pltpu.VMEM((count, rows, rows), jnp.bfloat16),
            pltpu.VMEM((count, rows, size), jnp.float32),
            pltpu.VMEM((count, size, 2 * size), jnp.float32),
        ],
        compiler_params=pltpu.CompilerParams(vmem_limit_bytes=48 * 2**20),
        cost_estimate=pl.CostEstimate(
            flops=count * 800 * size**3, bytes_accessed=count * 8 * size * size * 8, transcendentals=0
        ),
    )(side, gates, own0, own1, got0, got1, kept, sketch)


def from_partner(value):
    pairs = [(source, source ^ 1) for source in range(lax.axis_size("chain"))]
    return lax.ppermute(value, "chain", pairs)


def from_previous_site(value):
    groups, chain = lax.axis_size("group"), lax.axis_size("chain")
    at = [c * groups + g for g in range(groups) for c in range(chain)]
    return lax.ppermute(value, ("chain", "group"), list(zip(at[:-1], at[1:])))


def shift_next(values):
    return jnp.concatenate([values[1:], jnp.zeros_like(values[:1])], axis=0)


def shards(site_tensors, bond_weights, sector_sizes, kept_ranks, sketches, gate_ends, gate_pair):
    own_site = site_tensors[0, 0]
    nq, size = own_site.shape[:2]
    chain_at = lax.axis_index("chain")
    group_at = lax.axis_index("group")
    is_right = chain_at % 2 == 1
    column = lax.broadcasted_iota(jnp.int32, (nq, size), 1)
    own_lam = bond_weights[0, 0] * (column < sector_sizes[0, 0][:, None]).astype(jnp.float32)
    kept_own = (column < kept_ranks[0, 0][:, None]).astype(jnp.float32)
    message = from_previous_site(jnp.stack([own_lam, kept_own]))
    all_ones = jnp.ones((nq, size), jnp.float32)
    row_scale = jnp.where((chain_at == 0) & (group_at == 0), all_ones, message[0])
    kept_mask = jnp.where(is_right, message[1], kept_own)
    col_lam = jnp.where(is_right, own_lam, all_ones)
    col_next = shift_next(col_lam)

    def weigh(s, scale):
        value = own_site[:, :, s, :].astype(jnp.float32) * row_scale[:, :, None]
        return jnp.pad((value * scale[:, None, :]).astype(jnp.bfloat16), ((1, 1), (0, 0), (0, 0)))

    padded0, padded1 = weigh(0, col_lam), weigh(1, col_next)
    sectors = nq // 2
    each = sectors // CHUNKS
    send0 = jnp.where(is_right, 1, sectors)
    send1 = jnp.where(is_right, 0, sectors)
    mine0 = jnp.where(is_right, sectors + 1, 0)
    mine1 = jnp.where(is_right, sectors, 0)
    first = jnp.where(is_right, sectors, 0)
    cut = functools.partial(lax.dynamic_slice_in_dim, axis=0)

    side = is_right.astype(jnp.int32)[None]
    gates = jnp.concatenate([gate_ends, gate_pair])
    got = []
    for c in range(CHUNKS):
        low = 0 if c == 0 else c * each + 1
        length = (c + 1) * each + 1 - low
        got.append(from_partner((cut(padded0, send0 + low, length), cut(padded1, send1 + low, length))))
    kept_parts, back_parts = [], []
    for c in range(CHUNKS):
        if c == 0:
            got0, got1 = got[0]
        else:
            got0 = jnp.concatenate([got[c - 1][0][-1:], got[c][0]])
            got1 = jnp.concatenate([got[c - 1][1][-1:], got[c][1]])
        start = c * each
        keep, send = truncate(
            side,
            gates,
            cut(padded0, mine0 + start, each + 1),
            cut(padded1, mine1 + start, each + 1),
            got0,
            got1,
            cut(kept_mask, first + start, each)[:, None, :],
            cut(sketches, first + start, each),
        )
        kept_parts.append(keep)
        back_parts.append(from_partner(send))
    keep = jnp.concatenate(kept_parts)
    back = jnp.concatenate(back_parts)
    whole = jnp.where(
        is_right, jnp.concatenate([back, keep]), jnp.concatenate([keep, back])
    )
    second = jnp.where(is_right, whole[:, 1], shift_next(whole[:, 1]))
    return jnp.stack([whole[:, 0], second], axis=2)[None, None]


def solution(mesh):
    return jax.shard_map(
        shards,
        mesh=mesh,
        in_specs=(
            P("group", "chain", None, None, None, None),
            P("group", "chain", None, None),
            P("group", "chain", None),
            P("group", "chain", None),
            P(),
            P(),
            P(),
        ),
        out_specs=P("group", "chain", None, None, None, None),
        check_vma=False,
    )
```
